256 devices in a mesh: code: 128 (over y, z, x_lo, core), dp: 2 (over x_hi).
Axes of the slice: x: 4 (x_hi: 2, x_lo: 2; x = x_hi * 2 + x_lo), y: 4, z: 8, core: 2. Of those that a mesh axis runs over, the one named last changes fastest.
Arguments:
- latents: bfloat16 [2, 4096, 256], P('dp', 'code'), may hold values from -24 to 24
- codebook: bfloat16 [131072, 256], P('code'), may hold values from -0.7 to 0.7
- cotangent: bfloat16 [2, 4096, 256], P('dp', 'code'), may hold values from -6 to 6
Outputs:
- quantized: bfloat16 [2, 4096, 256], P('dp', 'code')
- code_grad: float32 [131072, 256], P('code')
The draws below stay inside these ranges and needn't reach their ends.
All inputs are finite; a program needn't handle non-finite values.
Results may differ from the reference program's by a relative error of at most 0.0095.
Values may be sent and summed in bfloat16 or wider, within the bound.
A program may use at most 128 MiB of HBM per device.

```python
import jax
import jax.numpy as jnp
from jax import lax

E = 256
CODES_DEV = 1024
K = 131072
TOKENS = 4096
GROUPS = 2
N_CODE = 128


def code_row(row_key, index):
    return jnp.clip(jax.random.normal(jax.random.fold_in(row_key, index), (E,), jnp.float32), -4.0, 4.0) * 0.15


def draw_codebook(key, part):
    row_key = jax.random.fold_in(key, 1)
    indices = jnp.arange(K)
    base = jax.vmap(lambda index: code_row(row_key, index))(indices)
    return base.astype(jnp.bfloat16)


def draw_latents(key, part):
    shape = (GROUPS, TOKENS, E)
    return jnp.clip(jax.random.normal(jax.random.fold_in(key, 4), shape, jnp.float32), -6.0, 6.0).astype(jnp.bfloat16)


def block_levels(stream_key, shape, shards, least, largest):
    factor_of, own = 1.0, jax.random.fold_in(stream_key, 6)
    for position, shards_of in shards:
        heights = jnp.exp(jax.random.uniform(jax.random.fold_in(own, position), (shards_of,), jnp.float32, least / len(shards), largest / len(shards)))
        factor_of = factor_of * jnp.repeat(heights, shape[position] // shards_of).reshape([-1 if axis == position else 1 for axis in range(len(shape))])
    return factor_of


def bell_draw(own_key, shape, scale, most, split=(), held_as=jnp.bfloat16):
    entries = scale * jax.random.normal(own_key, shape, jnp.float32)
    if split:
        entries = entries * block_levels(own_key, shape, split, -0.22, 0.18)
    return jnp.clip(entries, -most, most).astype(held_as)


def setup_inputs(seed: int = 0) -> dict:
    key_list = jax.random.split(jax.random.key(seed), 4)
    latents = draw_latents(jax.random.fold_in(key_list[3], 71), 0)
    codebook = draw_codebook(jax.random.fold_in(key_list[3], 71), 0)
    cotangent = bell_draw(key_list[2], (GROUPS, TOKENS, E), 1.0, 6.0, ((0, 2), (1, 128)))
    return {"latents": latents, "codebook": codebook, "cotangent": cotangent}


def block_logits(lat, block):
    block32 = block.astype(jnp.float32)
    half = 0.5 * jnp.sum(block32 * block32, axis=1)
    scores = lax.dot_general(lat, block, (((1,), (1,)), ((), ())), preferred_element_type=jnp.float32)
    return scores - half[None, :]


def reference(latents, codebook, cotangent):
    blocks = codebook.reshape(N_CODE, CODES_DEV, E)
    grad_total = jnp.zeros((N_CODE, CODES_DEV, E), jnp.float32)
    results = []
    contract = (((0,), (0,)), ((), ()))
    for replica in range(GROUPS):
        lat = latents[replica]
        cot = cotangent[replica]
        tops = lax.map(lambda block: jnp.max(block_logits(lat, block), axis=1), blocks)
        top = jnp.max(tops, axis=0)

        def accum(carry, block):
            total, mixed = carry
            expo = jnp.exp(block_logits(lat, block) - top[:, None])
            mixed = mixed + jnp.dot(expo.astype(jnp.bfloat16), block, preferred_element_type=jnp.float32)
            return (total + jnp.sum(expo, axis=1), mixed), None

        start = (jnp.zeros((TOKENS,), jnp.float32), jnp.zeros((TOKENS, E), jnp.float32))
        (total, mixed), unused = lax.scan(accum, start, blocks)
        quant = mixed / total[:, None]
        results.append(quant.astype(jnp.bfloat16))
        inner = jnp.sum(cot.astype(jnp.float32) * quant, axis=1)

        def grad_block(block):
            expo = jnp.exp(block_logits(lat, block) - top[:, None])
            prob = expo / total[:, None]
            align = lax.dot_general(cot, block, (((1,), (1,)), ((), ())), preferred_element_type=jnp.float32)
            slope = prob * (align - inner[:, None])
            first = lax.dot_general(prob.astype(jnp.bfloat16), cot, contract, preferred_element_type=jnp.float32)
            second = lax.dot_general(slope.astype(jnp.bfloat16), lat, contract, preferred_element_type=jnp.float32)
            return first + second - jnp.sum(slope, axis=0)[:, None] * block.astype(jnp.float32)

        grad_total = grad_total + lax.map(grad_block, blocks)
    scale = (K * 1.0) / (GROUPS * TOKENS)
    return jnp.stack(results), (grad_total * scale).reshape(K, E)
```

```python
import functools

import jax
import jax.numpy as jnp
from jax import lax
from jax.experimental import pallas as pl
from jax.experimental.pallas import tpu as pltpu
from jax.sharding import PartitionSpec as P

MESH = pl.DeviceIdType.MESH
NY, NZ, NX, NC = 4, 8, 2, 2
NB = NY * NX
NPLANE = NB * NC
BF, F32 = jnp.bfloat16, jnp.float32
CHUNK = 256
BY_LANE = (((1,), (1,)), ((), ()))


def kernel(
    scale, lat_ref, cb_ref, cot_ref, q_ref, g_ref,
    rows, expo, align, mixed, code_t, half, stats, zparts, pparts, final, gain,
    qpart, qcore, qy, qysum, qx, qxsum, qz, acc, slope_sum, gown, gin,
    ag_s, ag_r, ring_s, ring_r, sib_s, sib_r, zs_s, zs_r, pp_s, pp_r, za_s, za_r,
    qc_s, qc_r, qy_s, qy_r, qx_s, qx_r, qz_s, qz_r, dp_s, dp_r,
):
    me = lax.axis_index("code")
    rep = lax.axis_index("dp")
    c = me % NC
    x = (me // NC) % NX
    z = (me // (NC * NX)) % NZ
    y = me // (NC * NX * NZ)
    b = y * NX + x
    q = b * NC + c
    own = lat_ref.shape[0]
    tile = NB * own
    n_codes, width = cb_ref.shape
    n_chunks = n_codes // CHUNK

    def dev(y_, z_, x_, c_):
        return {"code": ((y_ * NZ + z_) * NX + x_) * NC + c_}

    def send(src, dst, s_sem, r_sem, device):
        return pltpu.make_async_remote_copy(
            src_ref=src, dst_ref=dst, send_sem=s_sem, recv_sem=r_sem,
            device_id=device, device_id_type=MESH,
        )

    def plane_dev(p_):
        b_ = p_ // NC
        return dev(b_ // NX, z, b_ % NX, p_ % NC)

    sibling = dev(y, z, x, 1 - c)
    other_dp = {"dp": 1 - rep}

    barrier = pltpu.get_barrier_semaphore()
    for d in range(1, NPLANE):
        pl.semaphore_signal(barrier, inc=1, device_id=plane_dev((q + d) % NPLANE), device_id_type=MESH)
    for d in range(1, NZ):
        pl.semaphore_signal(barrier, inc=1, device_id=dev(y, (z + d) % NZ, x, c), device_id_type=MESH)
    pl.semaphore_signal(barrier, inc=1, device_id=other_dp, device_id_type=MESH)

    own_rows = pl.ds(pl.multiple_of(b * own, own), own)
    rows[z, c, 0, own_rows, :] = lat_ref[...]
    rows[z, c, 1, own_rows, :] = cot_ref[...]

    pl.semaphore_wait(barrier, NPLANE - 1 + NZ - 1 + 1)

    def gather_copy(d):
        b_ = (b + d) % NB
        block = rows.at[z, c, :, own_rows, :]
        return send(block, block, ag_s.at[d], ag_r.at[d], dev(b_ // NX, z, b_ % NX, c))

    for d in range(1, NB):
        gather_copy(d).start()

    for k in range(n_chunks):
        part = cb_ref[k * CHUNK:(k + 1) * CHUNK, :].astype(F32)
        norm = 0.5 * jnp.sum(part * part, axis=1, keepdims=True)
        half[k * CHUNK:(k + 1) * CHUNK, :] = jnp.broadcast_to(norm, (CHUNK, tile))
        code_t[:, k * CHUNK:(k + 1) * CHUNK] = jnp.transpose(part).astype(BF)

    def gather_wait(d):
        b_ = (b + NB - d) % NB
        block = rows.at[z, c, :, pl.ds(pl.multiple_of(b_ * own, own), own), :]
        send(block, block, ag_s.at[d], ag_r.at[d], dev(y, z, x, 1 - c)).wait_recv()

    for d in range(1, NB):
        gather_wait(d)

    def zat(direction, step):
        return (z + NZ - step) % NZ if direction == 0 else (z + step) % NZ

    def ring_copy(direction, step, f):
        block = rows.at[zat(direction, step - 1), c, f]
        to = (z + 1) % NZ if direction == 0 else (z + NZ - 1) % NZ
        return send(block, block, ring_s.at[direction, step, f], ring_r.at[direction, step, f], dev(y, to, x, c))

    def ring_wait(direction, step, f):
        block = rows.at[zat(direction, step), c, f]
        send(block, block, ring_s.at[direction, step, f], ring_r.at[direction, step, f], sibling).wait_recv()

    def sib_copy(direction, step, f):
        block = rows.at[zat(direction, step), c, f]
        return send(block, block, sib_s.at[direction, step, f], sib_r.at[direction, step, f], sibling)

    def sib_wait(direction, step, f):
        block = rows.at[zat(direction, step), 1 - c, f]
        send(block, block, sib_s.at[direction, step, f], sib_r.at[direction, step, f], sibling).wait_recv()

    def scatter_copy(d):
        to = (z + d) % NZ
        return send(stats.at[to], zparts.at[z], zs_s.at[d], zs_r.at[d], dev(y, to, x, c))

    def tile_forward(zp, cp):
        lat = rows[zp, cp, 0]
        cot = rows[zp, cp, 1]
        top8 = None
        for k in range(n_chunks):
            ks = slice(k * CHUNK, (k + 1) * CHUNK)
            code = cb_ref[ks, :]
            logit = lax.dot_general(code, lat, BY_LANE, preferred_element_type=F32) - half[ks, :]
            expo[zp, cp, ks, :] = logit
            align[zp, cp, ks, :] = lax.dot_general(code, cot, BY_LANE, preferred_element_type=F32)
            part = jnp.max(logit.reshape(CHUNK // 8, 8, tile), axis=0)
            top8 = part if top8 is None else jnp.maximum(top8, part)
        top = jnp.max(top8, axis=0, keepdims=True)
        total8 = jnp.zeros((8, tile), F32)
        inner8 = jnp.zeros((8, tile), F32)
        mix = jnp.zeros((width, tile), F32)
        for k in range(n_chunks):
            ks = slice(k * CHUNK, (k + 1) * CHUNK)
            e = jnp.exp(expo[zp, cp, ks, :] - top)
            expo[zp, cp, ks, :] = e
            total8 += jnp.sum(e.reshape(CHUNK // 8, 8, tile), axis=0)
            inner8 += jnp.sum((e * align[zp, cp, ks, :]).reshape(CHUNK // 8, 8, tile), axis=0)
            mix += jnp.dot(code_t[:, ks], e.astype(BF), preferred_element_type=F32)
        mixed[zp, cp] = mix
        total = jnp.sum(total8, axis=0, keepdims=True)
        inner = jnp.sum(inner8, axis=0, keepdims=True)
        stats[zp, cp] = jnp.concatenate([top, total, inner, inner], axis=0)

    for f in range(2):
        for direction in range(2):
            ring_copy(direction, 1, f).start()
        sib_copy(0, 0, f).start()
    last = NZ // 2

    @pl.loop(0, 2)
    def _(j):
        @pl.when(j == 1)
        def _():
            sib_wait(0, 0, 0)
            sib_wait(0, 0, 1)
        tile_forward(z, (c + j) % 2)

    zparts[z] = stats[z]

    @pl.loop(1, last)
    def _(s):
        for f in range(2):
            for direction in range(2):
                ring_wait(direction, s, f)
                if direction == f:
                    ring_copy(direction, s + 1, f).start()
                else:
                    @pl.when(s + 1 < last)
                    def _():
                        ring_copy(direction, s + 1, f).start()
                sib_copy(direction, s, f).start()

        @pl.loop(0, 4)
        def _(j):
            @pl.when(j == 2)
            def _():
                for f in range(2):
                    for direction in range(2):
                        sib_wait(direction, s, f)
            zp = jnp.where(j % 2 == 0, (z + NZ - s) % NZ, (z + s) % NZ)
            tile_forward(zp, (c + j // 2) % 2)

        scatter_copy(NZ - s).start()
        scatter_copy(s).start()

    ring_wait(0, last, 0)
    sib_copy(0, last, 0).start()
    ring_wait(1, last, 1)
    sib_copy(1, last, 1).start()

    @pl.loop(0, 2)
    def _(j):
        @pl.when(j == 1)
        def _():
            sib_wait(0, last, 0)
            sib_wait(1, last, 1)
        tile_forward((z + last) % NZ, (c + j) % 2)

    scatter_copy(last).start()

    def combine(parts, n, cp):
        top = parts[0, cp, 0:1, :]
        for j in range(1, n):
            top = jnp.maximum(top, parts[j, cp, 0:1, :])
        total = jnp.zeros_like(top)
        inner = jnp.zeros_like(top)
        for j in range(n):
            w = jnp.exp(parts[j, cp, 0:1, :] - top)
            total += w * parts[j, cp, 1:2, :]
            inner += w * parts[j, cp, 2:3, :]
        return top, total, inner

    for d in range(1, NZ):
        part = zparts.at[(z + NZ - d) % NZ]
        send(part, part, zs_s.at[d], zs_r.at[d], sibling).wait_recv()
    for cp in range(2):
        top, total, inner = combine(zparts, NZ, cp)
        pparts[q, cp] = jnp.concatenate([top, total, inner, inner], axis=0)

    def plane_copy(d):
        return send(pparts.at[q], pparts.at[q], pp_s.at[d], pp_r.at[d], plane_dev((q + d) % NPLANE))

    for d in range(1, NPLANE):
        plane_copy(d).start()
    for d in range(1, NPLANE):
        part = pparts.at[(q + NPLANE - d) % NPLANE]
        send(part, part, pp_s.at[d], pp_r.at[d], sibling).wait_recv()
    for cp in range(2):
        top, total, inner = combine(pparts, NPLANE, cp)
        inverse = 1.0 / total
        final[z, cp] = jnp.concatenate([top, inverse, inner * inverse, inner], axis=0)

    def final_copy(d):
        return send(final.at[z], final.at[z], za_s.at[d], za_r.at[d], dev(y, (z + d) % NZ, x, c))

    for d in range(1, NZ):
        final_copy(d).start()
    for d in range(1, NZ):
        part = final.at[(z + NZ - d) % NZ]
        send(part, part, za_s.at[d], za_r.at[d], sibling).wait_recv()

    def quant_tile(zp, cp):
        share = jnp.exp(stats[zp, cp, 0:1, :] - final[zp, cp, 0:1, :]) * final[zp, cp, 1:2, :]
        gain[zp, cp] = jnp.concatenate([share, final[zp, cp, 2:3, :], share, share], axis=0)
        qpart[cp, zp] = jnp.transpose(mixed[zp, cp] * share).astype(BF)

    @pl.loop(0, NZ)
    def _(zp):
        quant_tile(zp, 1 - c)

    core_copy = send(qpart.at[1 - c], qcore, qc_s.at[0], qc_r.at[0], sibling)
    core_copy.start()

    @pl.loop(0, NZ)
    def _(zp):
        quant_tile(zp, c)

    def dp_copy(k):
        return send(gown.at[k], gin.at[k], dp_s.at[k], dp_r.at[k], other_dp)

    def grad_chunk(k):
        ks = pl.ds(pl.multiple_of(k * CHUNK, CHUNK), CHUNK)
        acc[...] = jnp.zeros_like(acc)
        slope_sum[...] = jnp.zeros_like(slope_sum)

        @pl.loop(0, NZ)
        def _(zp):
            out = acc[...]
            slopes = slope_sum[...]
            for cp in range(2):
                prob = expo[zp, cp, ks, :] * gain[zp, cp, 0:1, :]
                slope = prob * (align[zp, cp, ks, :] - gain[zp, cp, 1:2, :])
                out += jnp.dot(prob.astype(BF), rows[zp, cp, 1], preferred_element_type=F32)
                out += jnp.dot(slope.astype(BF), rows[zp, cp, 0], preferred_element_type=F32)
                slopes += slope
            acc[...] = out
            slope_sum[...] = slopes

        moved = jnp.sum(slope_sum[...], axis=1, keepdims=True) * cb_ref[ks, :].astype(F32)
        gown[k] = (acc[...] - moved).astype(BF)
        dp_copy(k).start()

    @pl.loop(0, 1)
    def _(k):
        grad_chunk(k)

    core_copy.wait()

    @pl.loop(0, NZ)
    def _(zp):
        qpart[c, zp] = (qpart[c, zp].astype(F32) + qcore[zp].astype(F32)).astype(BF)

    pair = NX * own

    def y_copy(d):
        to = (y + d) % NY
        part = qpart.at[c, :, pl.ds(pl.multiple_of(to * pair, pair), pair), :]
        return send(part, qy.at[d - 1], qy_s.at[d], qy_r.at[d], dev(to, z, x, c))

    for d in range(1, NY):
        y_copy(d).start()

    @pl.loop(1, n_chunks)
    def _(k):
        grad_chunk(k)

    for d in range(1, NY):
        y_copy(d).wait_recv()
    mine = pl.ds(pl.multiple_of(y * pair, pair), pair)
    total = qpart[c, :, mine, :].astype(F32)
    for d in range(NY - 1):
        total += qy[d].astype(F32)
    qysum[...] = total.astype(BF)
    x_copy = send(qysum.at[:, pl.ds(pl.multiple_of((1 - x) * own, own), own), :], qx, qx_s.at[0], qx_r.at[0], dev(y, z, 1 - x, c))
    x_copy.start()
    x_copy.wait_recv()
    mine = pl.ds(pl.multiple_of(x * own, own), own)
    qxsum[...] = (qysum[:, mine, :].astype(F32) + qx[...].astype(F32)).astype(BF)

    def z_copy(d):
        to = (z + d) % NZ
        return send(qxsum.at[to], qz.at[d - 1], qz_s.at[d], qz_r.at[d], dev(y, to, x, c))

    for d in range(1, NZ):
        z_copy(d).start()
    for d in range(1, NZ):
        z_copy(d).wait_recv()
    quant = qxsum[z].astype(F32)
    for d in range(NZ - 1):
        quant += qz[d].astype(F32)
    q_ref[...] = quant.astype(BF)

    @pl.loop(0, n_chunks)
    def _(k):
        dp_copy(k).wait_recv()
        ks = pl.ds(pl.multiple_of(k * CHUNK, CHUNK), CHUNK)
        g_ref[ks, :] = (gown[k].astype(F32) + gin[k].astype(F32)) * scale

    for d in range(1, NB):
        gather_copy(d).wait_send()
    for f in range(2):
        sib_copy(0, 0, f).wait_send()
        for direction in range(2):
            @pl.loop(1, last)
            def _(s):
                ring_copy(direction, s, f).wait_send()
                sib_copy(direction, s, f).wait_send()
        ring_copy(f, last, f).wait_send()
        sib_copy(f, last, f).wait_send()
    for d in range(1, NZ):
        scatter_copy(d).wait_send()
        final_copy(d).wait_send()
        z_copy(d).wait_send()
    for d in range(1, NPLANE):
        plane_copy(d).wait_send()
    for d in range(1, NY):
        y_copy(d).wait_send()
    x_copy.wait_send()

    @pl.loop(0, n_chunks)
    def _(k):
        dp_copy(k).wait_send()


def body(latents, codebook, cotangent):
    own, width = latents.shape[1:]
    n_codes = codebook.shape[0]
    tile = NB * own
    n_chunks = n_codes // CHUNK
    n_tokens = own * lax.axis_size("code")
    scale = n_codes * lax.axis_size("code") * 1.0 / (lax.axis_size("dp") * n_tokens)
    vmem = pl.BlockSpec(memory_space=pltpu.VMEM)
    dma = pltpu.SemaphoreType.DMA
    half_ring = NZ // 2 + 1
    quantized, grad = pl.pallas_call(
        functools.partial(kernel, scale),
        out_shape=(
            jax.ShapeDtypeStruct((own, width), BF),
            jax.ShapeDtypeStruct((n_codes, width), F32),
        ),
        in_specs=[vmem] * 3,
        out_specs=(vmem, vmem),
        scratch_shapes=[
            pltpu.VMEM((NZ, NC, 2, tile, width), BF),
            pltpu.VMEM((NZ, NC, n_codes, tile), F32),
            pltpu.VMEM((NZ, NC, n_codes, tile), F32),
            pltpu.VMEM((NZ, NC, width, tile), F32),
            pltpu.VMEM((width, n_codes), BF),
            pltpu.VMEM((n_codes, tile), F32),
            pltpu.VMEM((NZ, NC, 4, tile), F32),
            pltpu.VMEM((NZ, NC, 4, tile), F32),
            pltpu.VMEM((NPLANE, NC, 4, tile), F32),
            pltpu.VMEM((NZ, NC, 4, tile), F32),
            pltpu.VMEM((NZ, NC, 4, tile), F32),
            pltpu.VMEM((NC, NZ, tile, width), BF),
            pltpu.VMEM((NZ, tile, width), BF),
            pltpu.VMEM((NY - 1, NZ, NX * own, width), BF),
            pltpu.VMEM((NZ, NX * own, width), BF),
            pltpu.VMEM((NZ, own, width), BF),
            pltpu.VMEM((NZ, own, width), BF),
            pltpu.VMEM((NZ - 1, own, width), BF),
            pltpu.VMEM((CHUNK, width), F32),
            pltpu.VMEM((CHUNK, tile), F32),
            pltpu.VMEM((n_chunks, CHUNK, width), BF),
            pltpu.VMEM((n_chunks, CHUNK, width), BF),
            dma((NB,)), dma((NB,)),
            dma((2, half_ring, 2)), dma((2, half_ring, 2)),
            dma((2, half_ring, 2)), dma((2, half_ring, 2)),
            dma((NZ,)), dma((NZ,)),
            dma((NPLANE,)), dma((NPLANE,)),
            dma((NZ,)), dma((NZ,)),
            dma((1,)), dma((1,)),
            dma((NY,)), dma((NY,)),
            dma((1,)), dma((1,)),
            dma((NZ,)), dma((NZ,)),
            dma((n_chunks,)), dma((n_chunks,)),
        ],
        compiler_params=pltpu.CompilerParams(
            collective_id=0, has_side_effects=True, vmem_limit_bytes=60 * 1024 * 1024,
        ),
        cost_estimate=pl.CostEstimate(
            flops=10 * n_codes * n_tokens * width, bytes_accessed=4 * n_codes * width,
            transcendentals=n_codes * n_tokens,
        ),
    )(latents[0], codebook, cotangent[0])
    return quantized[None], grad


def solution(mesh):
    in_specs = (P("dp", "code", None), P("code", None), P("dp", "code", None))
    out_specs = (P("dp", "code", None), P("code", None))
    return jax.shard_map(body, mesh=mesh, in_specs=in_specs, out_specs=out_specs, check_vma=False)
```

```python
import jax
import jax.numpy as jnp
from jax import lax
from jax.experimental import pallas as pl
from jax.experimental.pallas import tpu as pltpu
from jax.sharding import PartitionSpec as P

MESH = pl.DeviceIdType.MESH
NY, NZ, NX, NC = 4, 8, 2, 2
NB = NY * NX
BF, F32 = jnp.bfloat16, jnp.float32
CHUNK = 256
BY_LANE = (((1,), (1,)), ((), ()))


def kernel(
    lat_ref, cb_ref, cot_ref, q_ref, gown_ref, gin_ref,
    rows, expo, align, mixed, code_t, half, stats, pstats, smix, pmix, pairs, zparts, bparts, final, gain,
    qpart, qplane, qsend, qz, acc, slope_sum, gin,
    ag_s, ag_r, ring_s, ring_r, sib_s, sib_r, pm_s, pm_r, ps_s, ps_r, zs_s, zs_r, bp_s, bp_r, za_s, za_r, fin_s, fin_r,
    qp_s, qp_r, qz_s, qz_r, dp_s, dp_r,
):
    me = lax.axis_index("code")
    rep = lax.axis_index("dp")
    c = me % NC
    x = (me // NC) % NX
    z = (me // (NC * NX)) % NZ
    y = me // (NC * NX * NZ)
    b = y * NX + x
    own = lat_ref.shape[0]
    tile = NB * own
    n_codes, width = cb_ref.shape
    n_chunks = n_codes // CHUNK

    def dev(y_, z_, x_, c_):
        return {"code": ((y_ * NZ + z_) * NX + x_) * NC + c_}

    def send(src, dst, s_sem, r_sem, device):
        return pltpu.make_async_remote_copy(
            src_ref=src, dst_ref=dst, send_sem=s_sem, recv_sem=r_sem,
            device_id=device, device_id_type=MESH,
        )

    def block_dev(b_):
        return dev(b_ // NX, z, b_ % NX, c)

    sibling = dev(y, z, x, 1 - c)
    other_dp = {"dp": 1 - rep}

    def wait_in(ref, r_sem):
        send(ref, ref, r_sem, r_sem, sibling).wait_recv()

    barrier = pltpu.get_barrier_semaphore()
    pl.semaphore_signal(barrier, inc=1, device_id=sibling, device_id_type=MESH)
    pl.semaphore_signal(barrier, inc=1, device_id=other_dp, device_id_type=MESH)
    for d in range(1, NB):
        pl.semaphore_signal(barrier, inc=1, device_id=block_dev((b + d) % NB), device_id_type=MESH)
    for d in range(1, NZ):
        pl.semaphore_signal(barrier, inc=1, device_id=dev(y, (z + d) % NZ, x, c), device_id_type=MESH)

    own_rows = pl.ds(pl.multiple_of(b * own, own), own)
    rows[z, c, 0, own_rows, :] = lat_ref[...]
    rows[z, c, 1, own_rows, :] = cot_ref[...]

    for k in range(n_chunks):
        part = cb_ref[k * CHUNK:(k + 1) * CHUNK, :].astype(F32)
        norm = 0.5 * jnp.sum(part * part, axis=1, keepdims=True)
        half[k * CHUNK:(k + 1) * CHUNK, :] = jnp.broadcast_to(norm, (CHUNK, tile))
        code_t[:, k * CHUNK:(k + 1) * CHUNK] = jnp.transpose(part).astype(BF)

    pl.semaphore_wait(barrier, 2 + NB - 1 + NZ - 1)

    def gather_copy(d):
        block = rows.at[z, c, :, own_rows, :]
        return send(block, block, ag_s.at[d], ag_r.at[d], block_dev((b + d) % NB))

    for d in range(1, NB):
        gather_copy(d).start()

    for d in range(1, NB):
        b_ = (b + NB - d) % NB
        wait_in(rows.at[z, c, :, pl.ds(pl.multiple_of(b_ * own, own), own), :], ag_r.at[d])

    last = NZ // 2

    def zat(direction, step):
        return (z + NZ - step) % NZ if direction == 0 else (z + step) % NZ

    def ring_copy(direction, step, f):
        block = rows.at[zat(direction, step - 1), c, f]
        to = (z + 1) % NZ if direction == 0 else (z + NZ - 1) % NZ
        return send(block, block, ring_s.at[direction, step, f], ring_r.at[direction, step, f], dev(y, to, x, c))

    def sib_copy(direction, step, f):
        block = rows.at[zat(direction, step), c, f]
        return send(block, block, sib_s.at[direction, step, f], sib_r.at[direction, step, f], sibling)

    def sib_wait(direction, step, f):
        wait_in(rows.at[zat(direction, step), 1 - c, f], sib_r.at[direction, step, f])

    def arrivals(step):
        if step == 0:
            return [(0, 0), (0, 1)]
        if step == last:
            return [(0, 0), (1, 1)]
        return [(direction, f) for f in range(2) for direction in range(2)]

    def planes(step, run):
        if step == 0 or step == last:
            run((z + step) % NZ)
        else:
            @pl.loop(0, 2)
            def _(j):
                run(jnp.where(j == 0, (z + NZ - step) % NZ, (z + step) % NZ))

    def tile_forward(zp, cp):
        lat = rows[zp, cp, 0]
        cot = rows[zp, cp, 1]
        top8 = None
        for k in range(n_chunks):
            ks = slice(k * CHUNK, (k + 1) * CHUNK)
            code = cb_ref[ks, :]
            logit = lax.dot_general(code, lat, BY_LANE, preferred_element_type=F32) - half[ks, :]
            expo[zp, cp, ks, :] = logit
            align[zp, cp, ks, :] = lax.dot_general(code, cot, BY_LANE, preferred_element_type=F32)
            part = jnp.max(logit.reshape(CHUNK // 8, 8, tile), axis=0)
            top8 = part if top8 is None else jnp.maximum(top8, part)
        top = jnp.max(top8, axis=0, keepdims=True)
        total8 = jnp.zeros((8, tile), F32)
        inner8 = jnp.zeros((8, tile), F32)
        mix = jnp.zeros((width, tile), F32)
        for k in range(n_chunks):
            ks = slice(k * CHUNK, (k + 1) * CHUNK)
            e = jnp.exp(expo[zp, cp, ks, :] - top)
            expo[zp, cp, ks, :] = e
            total8 += jnp.sum(e.reshape(CHUNK // 8, 8, tile), axis=0)
            inner8 += jnp.sum((e * align[zp, cp, ks, :]).reshape(CHUNK // 8, 8, tile), axis=0)
            mix += jnp.dot(code_t[:, ks], e.astype(BF), preferred_element_type=F32)
        mixed[zp, cp] = mix
        total = jnp.sum(total8, axis=0, keepdims=True)
        inner = jnp.sum(inner8, axis=0, keepdims=True)
        stats[zp, cp] = jnp.concatenate([top, total, inner, inner], axis=0)

    def combine(part, n):
        top = part(0)[0:1, :]
        for j in range(1, n):
            top = jnp.maximum(top, part(j)[0:1, :])
        total = jnp.zeros_like(top)
        inner = jnp.zeros_like(top)
        for j in range(n):
            p = part(j)
            w = jnp.exp(p[0:1, :] - top)
            total += w * p[1:2, :]
            inner += w * p[2:3, :]
        return top, total, inner

    def pair_mix_copy(zp):
        return send(smix.at[zp], pmix.at[zp], pm_s.at[zp], pm_r.at[zp], sibling)

    def pair_stat_copy(zp):
        return send(stats.at[zp, 1 - c], pstats.at[zp], ps_s.at[zp], ps_r.at[zp], sibling)

    def pair_send(zp):
        pair_stat_copy(zp).start()
        smix[zp] = mixed[zp, 1 - c].astype(BF)
        pair_mix_copy(zp).start()

    def scatter_copy(d):
        to = (z + d) % NZ
        return send(pairs.at[to], zparts.at[z], zs_s.at[d], zs_r.at[d], dev(y, to, x, c))

    def pair_stats(zp):
        pair_stat_copy(zp).wait_recv()
        mine, other = stats[zp, c], pstats[zp]
        top = jnp.maximum(mine[0:1, :], other[0:1, :])
        w0 = jnp.exp(mine[0:1, :] - top)
        w1 = jnp.exp(other[0:1, :] - top)
        total = mine[1:2, :] * w0 + other[1:2, :] * w1
        inner = mine[2:3, :] * w0 + other[2:3, :] * w1
        pairs[zp] = jnp.concatenate([top, total, inner, inner], axis=0)

    def pair_mix(zp):
        pair_mix_copy(zp).wait_recv()
        top = pairs[zp, 0:1, :]
        w0 = jnp.exp(stats[zp, c, 0:1, :] - top)
        w1 = jnp.exp(pstats[zp, 0:1, :] - top)
        mixed[zp, c] = mixed[zp, c] * w0 + pmix[zp].astype(F32) * w1

    def pair_step(step):
        planes(step, pair_stats)
        if step == 0:
            zparts[z] = pairs[z]
        else:
            scatter_copy(step).start()
            if step < last:
                scatter_copy(NZ - step).start()

    for step in range(last + 1):
        for direction, f in arrivals(step):
            if step > 0:
                wait_in(rows.at[zat(direction, step), c, f], ring_r.at[direction, step, f])
            if step == 0:
                ring_copy(0, 1, f).start()
                ring_copy(1, 1, f).start()
            elif (direction, f) in arrivals(step + 1) and step < last:
                ring_copy(direction, step + 1, f).start()
            sib_copy(direction, step, f).start()
        if step >= 1:
            pair_step(step - 1)
            planes(step - 1, pair_mix)

        single = step == 0 or step == last
        n = 1 if single else 2

        @pl.loop(0, 2 * n)
        def _(j):
            @pl.when(j == n)
            def _():
                for direction, f in arrivals(step):
                    sib_wait(direction, step, f)
            zp = (z + step) % NZ
            if not single:
                zp = jnp.where(j % 2 == 0, (z + NZ - step) % NZ, zp)
            tile_forward(zp, (c + j // n) % 2)

        planes(step, pair_send)

    pair_step(last)

    for d in range(1, NZ):
        wait_in(zparts.at[(z + NZ - d) % NZ], zs_r.at[d])
    top, total, inner = combine(lambda j: zparts[j], NZ)
    bparts[b] = jnp.concatenate([top, total, inner, inner], axis=0)

    def block_copy(d):
        return send(bparts.at[b], bparts.at[b], bp_s.at[d], bp_r.at[d], block_dev((b + d) % NB))

    for d in range(1, NB):
        block_copy(d).start()
    planes(last, pair_mix)
    for d in range(1, NB):
        wait_in(bparts.at[(b + NB - d) % NB], bp_r.at[d])
    top, total, inner = combine(lambda j: bparts[j], NB)
    inverse = 1.0 / total
    final[c, z] = jnp.concatenate([top, inverse, inner * inverse, inner], axis=0)

    def back_copy(d):
        return send(final.at[c, z], final.at[c, z], za_s.at[d], za_r.at[d], dev(y, (z + d) % NZ, x, c))

    for d in range(1, NZ):
        back_copy(d).start()
    for d in range(1, NZ):
        wait_in(final.at[c, (z + NZ - d) % NZ], za_r.at[d])
    final_copy = send(final.at[c], final.at[c], fin_s.at[0], fin_r.at[0], sibling)
    final_copy.start()

    def set_gain(zp, cp):
        share = jnp.exp(stats[zp, cp, 0:1, :] - final[cp, zp, 0:1, :]) * final[cp, zp, 1:2, :]
        gain[zp, cp] = jnp.concatenate([share, final[cp, zp, 2:3, :], share, share], axis=0)

    @pl.loop(0, NZ)
    def _(zp):
        set_gain(zp, c)
        share = jnp.exp(pairs[zp, 0:1, :] - final[c, zp, 0:1, :]) * final[c, zp, 1:2, :]
        qpart[zp] = jnp.transpose(mixed[zp, c] * share).astype(BF)

    def quant_copy(d):
        b_ = (b + d) % NB
        part = qpart.at[:, pl.ds(pl.multiple_of(b_ * own, own), own), :]
        return send(part, qplane.at[d - 1], qp_s.at[d], qp_r.at[d], block_dev(b_))

    for d in range(1, NB):
        quant_copy(d).start()

    wait_in(final.at[1 - c], fin_r.at[0])

    @pl.loop(0, NZ)
    def _(zp):
        set_gain(zp, 1 - c)

    def dp_copy(k):
        return send(gown_ref.at[k], gin.at[k], dp_s.at[k], dp_r.at[k], other_dp)

    def grad_chunk(k):
        ks = pl.ds(pl.multiple_of(k * CHUNK, CHUNK), CHUNK)
        acc[...] = jnp.zeros_like(acc)
        slope_sum[...] = jnp.zeros_like(slope_sum)

        @pl.loop(0, NZ)
        def _(zp):
            out = acc[...]
            slopes = slope_sum[...]
            for cp in range(2):
                prob = expo[zp, cp, ks, :] * gain[zp, cp, 0:1, :]
                slope = prob * (align[zp, cp, ks, :] - gain[zp, cp, 1:2, :])
                out += jnp.dot(prob.astype(BF), rows[zp, cp, 1], preferred_element_type=F32)
                out += jnp.dot(slope.astype(BF), rows[zp, cp, 0], preferred_element_type=F32)
                slopes += slope
            acc[...] = out
            slope_sum[...] = slopes

        moved = jnp.sum(slope_sum[...], axis=1, keepdims=True) * cb_ref[ks, :].astype(F32)
        gown_ref[k] = (acc[...] - moved).astype(BF)
        dp_copy(k).start()

    def z_copy(d):
        to = (z + d) % NZ
        return send(qsend.at[to], qz.at[d - 1], qz_s.at[d], qz_r.at[d], dev(y, to, x, c))

    @pl.loop(0, n_chunks)
    def _(k):
        grad_chunk(k)

    for d in range(1, NB):
        quant_copy(d).wait_recv()
    total = qpart[:, own_rows, :].astype(F32)
    for d in range(NB - 1):
        total += qplane[d].astype(F32)
    qsend[...] = total.astype(BF)
    for d in range(1, NZ):
        z_copy(d).start()

    for d in range(1, NB):
        gather_copy(d).wait_send()
        block_copy(d).wait_send()
        quant_copy(d).wait_send()
    for step in range(last + 1):
        for direction, f in arrivals(step):
            if step > 0:
                ring_copy(direction, step, f).wait_send()
            sib_copy(direction, step, f).wait_send()
    for d in range(1, NZ):
        scatter_copy(d).wait_send()
        back_copy(d).wait_send()
    final_copy.wait_send()

    @pl.loop(0, NZ)
    def _(zp):
        pair_mix_copy(zp).wait_send()
        pair_stat_copy(zp).wait_send()

    @pl.loop(0, n_chunks)
    def _(k):
        dp_copy(k).wait()
        gin_ref[k] = gin[k]

    for d in range(1, NZ):
        z_copy(d).wait()
    quant = qsend[z].astype(F32)
    for d in range(NZ - 1):
        quant += qz[d].astype(F32)
    q_ref[...] = quant.astype(BF)


def body(latents, codebook, cotangent):
    own, width = latents.shape[1:]
    n_codes = codebook.shape[0]
    tile = NB * own
    n_chunks = n_codes // CHUNK
    n_tokens = own * lax.axis_size("code")
    scale = n_codes * lax.axis_size("code") * 1.0 / (lax.axis_size("dp") * n_tokens)
    vmem = pl.BlockSpec(memory_space=pltpu.VMEM)
    dma = pltpu.SemaphoreType.DMA
    half_ring = NZ // 2 + 1
    halves = jax.ShapeDtypeStruct((n_chunks, CHUNK, width), BF)
    quantized, here, there = pl.pallas_call(
        kernel,
        out_shape=(jax.ShapeDtypeStruct((own, width), BF), halves, halves),
        in_specs=[vmem] * 3,
        out_specs=(vmem, vmem, vmem),
        scratch_shapes=[
            pltpu.VMEM((NZ, NC, 2, tile, width), BF),
            pltpu.VMEM((NZ, NC, n_codes, tile), F32),
            pltpu.VMEM((NZ, NC, n_codes, tile), F32),
            pltpu.VMEM((NZ, NC, width, tile), F32),
            pltpu.VMEM((width, n_codes), BF),
            pltpu.VMEM((n_codes, tile), F32),
            pltpu.VMEM((NZ, NC, 4, tile), F32),
            pltpu.VMEM((NZ, 4, tile), F32),
            pltpu.VMEM((NZ, width, tile), BF),
            pltpu.VMEM((NZ, width, tile), BF),
            pltpu.VMEM((NZ, 4, tile), F32),
            pltpu.VMEM((NZ, 4, tile), F32),
            pltpu.VMEM((NB, 4, tile), F32),
            pltpu.VMEM((NC, NZ, 4, tile), F32),
            pltpu.VMEM((NZ, NC, 4, tile), F32),
            pltpu.VMEM((NZ, tile, width), BF),
            pltpu.VMEM((NB - 1, NZ, own, width), BF),
            pltpu.VMEM((NZ, own, width), BF),
            pltpu.VMEM((NZ - 1, own, width), BF),
            pltpu.VMEM((CHUNK, width), F32),
            pltpu.VMEM((CHUNK, tile), F32),
            pltpu.VMEM((n_chunks, CHUNK, width), BF),
            dma((NB,)), dma((NB,)),
            dma((2, half_ring, 2)), dma((2, half_ring, 2)),
            dma((2, half_ring, 2)), dma((2, half_ring, 2)),
            dma((NZ,)), dma((NZ,)),
            dma((NZ,)), dma((NZ,)),
            dma((NZ,)), dma((NZ,)),
            dma((NB,)), dma((NB,)),
            dma((NZ,)), dma((NZ,)),
            dma((1,)), dma((1,)),
            dma((NB,)), dma((NB,)),
            dma((NZ,)), dma((NZ,)),
            dma((n_chunks,)), dma((n_chunks,)),
        ],
        compiler_params=pltpu.CompilerParams(
            collective_id=0, has_side_effects=True, vmem_limit_bytes=60 * 1024 * 1024,
        ),
        cost_estimate=pl.CostEstimate(
            flops=10 * n_codes * n_tokens * width, bytes_accessed=4 * n_codes * width,
            transcendentals=n_codes * n_tokens,
        ),
    )(latents[0], codebook, cotangent[0])
    grad = (here.astype(F32) + there.astype(F32)) * scale
    return quantized[None], grad.reshape(n_codes, width)


def solution(mesh):
    in_specs = (P("dp", "code", None), P("code", None), P("dp", "code", None))
    out_specs = (P("dp", "code", None), P("code", None))
    return jax.shard_map(body, mesh=mesh, in_specs=in_specs, out_specs=out_specs, check_vma=False)
```

```python
import jax
import jax.numpy as jnp
from jax import lax
from jax.experimental import pallas as pl
from jax.experimental.pallas import tpu as pltpu
from jax.sharding import PartitionSpec as P

MESH = pl.DeviceIdType.MESH
NY, NZ, NX, NC = 4, 8, 2, 2
NB = NY * NX
BF, F32 = jnp.bfloat16, jnp.float32
CHUNK = 256
BY_LANE = (((1,), (1,)), ((), ()))


def kernel(
    lat_ref, cb_ref, cot_ref, q_ref, gown_ref, gin_ref,
    rows, expo, align, mixed, code_t, half, stats, pstats, smix, pmix, pairs, zparts, bparts, final, gain,
    qpart, qplane, qsend, qz, gin,
    ag_s, ag_r, zx_s, zx_r, col_s, col_r, ring_s, ring_r, sib_s, sib_r, pm_s, pm_r, ps_s, ps_r, zs_s, zs_r, bp_s, bp_r, za_s, za_r, fin_s, fin_r,
    qp_s, qp_r, qz_s, qz_r, dp_s, dp_r,
):
    me = lax.axis_index("code")
    rep = lax.axis_index("dp")
    c = me % NC
    x = (me // NC) % NX
    z = (me // (NC * NX)) % NZ
    y = me // (NC * NX * NZ)
    b = y * NX + x
    own = lat_ref.shape[0]
    tile = NB * own
    n_codes, width = cb_ref.shape
    n_chunks = n_codes // CHUNK

    def dev(y_, z_, x_, c_):
        return {"code": ((y_ * NZ + z_) * NX + x_) * NC + c_}

    def send(src, dst, s_sem, r_sem, device):
        return pltpu.make_async_remote_copy(
            src_ref=src, dst_ref=dst, send_sem=s_sem, recv_sem=r_sem,
            device_id=device, device_id_type=MESH,
        )

    def block_dev(b_):
        return dev(b_ // NX, z, b_ % NX, c)

    sibling = dev(y, z, x, 1 - c)
    other_dp = {"dp": 1 - rep}

    def wait_in(ref, r_sem):
        send(ref, ref, r_sem, r_sem, sibling).wait_recv()

    def wait_out(ref, s_sem):
        send(ref, ref, s_sem, s_sem, sibling).wait_send()

    barrier = pltpu.get_barrier_semaphore()
    pl.semaphore_signal(barrier, inc=1, device_id=sibling, device_id_type=MESH)
    pl.semaphore_signal(barrier, inc=1, device_id=other_dp, device_id_type=MESH)
    for d in range(1, NB):
        pl.semaphore_signal(barrier, inc=1, device_id=block_dev((b + d) % NB), device_id_type=MESH)
    for d in range(1, NZ):
        pl.semaphore_signal(barrier, inc=1, device_id=dev(y, (z + d) % NZ, x, c), device_id_type=MESH)

    own_rows = pl.ds(pl.multiple_of(b * own, own), own)
    rows[z, c, 0, own_rows, :] = lat_ref[...]
    rows[z, c, 1, own_rows, :] = cot_ref[...]

    for k in range(n_chunks):
        part = cb_ref[k * CHUNK:(k + 1) * CHUNK, :].astype(F32)
        norm = 0.5 * jnp.sum(part * part, axis=1, keepdims=True)
        half[k * CHUNK:(k + 1) * CHUNK, :] = jnp.broadcast_to(norm, (CHUNK, tile))

    pl.semaphore_wait(barrier, 2 + NB - 1 + NZ - 1)

    def gather_copy(d, f):
        block = rows.at[z, c, f, own_rows, :]
        return send(block, block, ag_s.at[d, f], ag_r.at[d, f], block_dev((b + d) % NB))

    def gather_wait(f):
        for d in range(1, NB):
            b_ = (b + NB - d) % NB
            wait_in(rows.at[z, c, f, pl.ds(pl.multiple_of(b_ * own, own), own), :], ag_r.at[d, f])

    def spread_copy(d):
        block = rows.at[z, c, :, own_rows, :]
        return send(block, block, zx_s.at[d], zx_r.at[d], dev(y, (z + d) % NZ, x, c))

    def column_send(zp):
        block = rows.at[zp, c, :, own_rows, :]
        for d in range(1, NB):
            send(block, block, col_s.at[zp], col_r.at[zp], block_dev((b + d) % NB)).start()

    def column_wait(zp):
        wait_in(rows.at[zp, c, :, 0:(NB - 1) * own, :], col_r.at[zp])

    @pl.when(c == 0)
    def _():
        for d in range(1, NB):
            gather_copy(d, 0).start()

    @pl.when(c == 1)
    def _():
        for d in range(1, NZ):
            spread_copy(d).start()

    for k in range(n_chunks):
        part = cb_ref[k * CHUNK:(k + 1) * CHUNK, :].astype(F32)
        code_t[:, k * CHUNK:(k + 1) * CHUNK] = jnp.transpose(part).astype(BF)

    @pl.when(c == 0)
    def _():
        for d in range(1, NB):
            gather_copy(d, 0).wait_send()
        for d in range(1, NB):
            gather_copy(d, 1).start()

    last = NZ // 2

    def zat(direction, step):
        return (z + NZ - step) % NZ if direction == 0 else (z + step) % NZ

    def ring_copy(direction, step, f):
        block = rows.at[zat(direction, step - 1), c, f]
        to = (z + 1) % NZ if direction == 0 else (z + NZ - 1) % NZ
        return send(block, block, ring_s.at[direction, step, f], ring_r.at[direction, step, f], dev(y, to, x, c))

    def sib_copy(zp):
        return send(rows.at[zp, c], rows.at[zp, c], sib_s.at[zp], sib_r.at[zp], sibling)

    def planes(step, run):
        if isinstance(step, int) and step in (0, last):
            run((z + step) % NZ)
        else:
            @pl.loop(0, jnp.minimum(step + 1, 2))
            def _(j):
                run(jnp.where(j == 0, (z + NZ - step) % NZ, (z + step) % NZ))

    def tile_forward(zp, cp):
        lat = rows[zp, cp, 0]
        cot = rows[zp, cp, 1]
        top8 = None
        for k in range(n_chunks):
            ks = slice(k * CHUNK, (k + 1) * CHUNK)
            code = cb_ref[ks, :]
            logit = lax.dot_general(code, lat, BY_LANE, preferred_element_type=F32) - half[ks, :]
            expo[zp, cp, ks, :] = logit
            align[zp, cp, ks, :] = lax.dot_general(code, cot, BY_LANE, preferred_element_type=F32)
            part = jnp.max(logit.reshape(CHUNK // 8, 8, tile), axis=0)
            top8 = part if top8 is None else jnp.maximum(top8, part)
        top = jnp.max(top8, axis=0, keepdims=True)
        total8 = jnp.zeros((8, tile), F32)
        inner8 = jnp.zeros((8, tile), F32)
        mix = jnp.zeros((width, tile), F32)
        for k in range(n_chunks):
            ks = slice(k * CHUNK, (k + 1) * CHUNK)
            e = jnp.exp(expo[zp, cp, ks, :] - top)
            expo[zp, cp, ks, :] = e
            total8 += jnp.sum(e.reshape(CHUNK // 8, 8, tile), axis=0)
            inner8 += jnp.sum((e * align[zp, cp, ks, :]).reshape(CHUNK // 8, 8, tile), axis=0)
            mix += jnp.dot(code_t[:, ks], e.astype(BF), preferred_element_type=F32)
        mixed[zp, cp] = mix
        total = jnp.sum(total8, axis=0, keepdims=True)
        inner = jnp.sum(inner8, axis=0, keepdims=True)
        stats[zp, cp] = jnp.concatenate([top, total, inner, inner], axis=0)

    def combine(part, n):
        top = part(0)[0:1, :]
        for j in range(1, n):
            top = jnp.maximum(top, part(j)[0:1, :])
        total = jnp.zeros_like(top)
        inner = jnp.zeros_like(top)
        for j in range(n):
            p = part(j)
            w = jnp.exp(p[0:1, :] - top)
            total += w * p[1:2, :]
            inner += w * p[2:3, :]
        return top, total, inner

    def pair_mix_copy(zp):
        return send(smix.at[zp], pmix.at[zp], pm_s.at[zp], pm_r.at[zp], sibling)

    def pair_stat_copy(zp):
        return send(stats.at[zp, 1 - c], pstats.at[zp], ps_s.at[zp], ps_r.at[zp], sibling)

    def pair_send(zp):
        pair_stat_copy(zp).start()
        smix[zp] = mixed[zp, 1 - c].astype(BF)
        pair_mix_copy(zp).start()

    def scatter_copy(d):
        to = (z + d) % NZ
        return send(pairs.at[to], zparts.at[z], zs_s.at[d], zs_r.at[d], dev(y, to, x, c))

    def pair_stats(zp):
        pair_stat_copy(zp).wait_recv()
        mine, other = stats[zp, c], pstats[zp]
        top = jnp.maximum(mine[0:1, :], other[0:1, :])
        w0 = jnp.exp(mine[0:1, :] - top)
        w1 = jnp.exp(other[0:1, :] - top)
        total = mine[1:2, :] * w0 + other[1:2, :] * w1
        inner = mine[2:3, :] * w0 + other[2:3, :] * w1
        pairs[zp] = jnp.concatenate([top, total, inner, inner], axis=0)

    def pair_mix(zp):
        pair_mix_copy(zp).wait_recv()
        top = pairs[zp, 0:1, :]
        w0 = jnp.exp(stats[zp, c, 0:1, :] - top)
        w1 = jnp.exp(pstats[zp, 0:1, :] - top)
        mixed[zp, c] = mixed[zp, c] * w0 + pmix[zp].astype(F32) * w1

    def pair_step(step):
        planes(step, pair_stats)

        @pl.when(step == 0)
        def _():
            zparts[z] = pairs[z]

        @pl.when(step > 0)
        def _():
            scatter_copy(step).start()

        @pl.when((step > 0) & (step < last))
        def _():
            scatter_copy(NZ - step).start()

    def own_tiles(step):
        planes(step, lambda zp: tile_forward(zp, c))

    def sib_tiles(step):
        def run(zp):
            wait_in(rows.at[zp, 1 - c], sib_r.at[zp])
            tile_forward(zp, 1 - c)
            pair_send(zp)

        planes(step, run)

    def ring_wait(direction, step, f):
        wait_in(rows.at[zat(direction, step), c, f], ring_r.at[direction, step, f])

    @pl.when(c == 0)
    def _():
        for f in range(2):
            gather_wait(f)
            for direction in range(2):
                ring_copy(direction, 1, f).start()

    @pl.when(c == 1)
    def _():
        for d in range(1, NZ):
            block = rows.at[(z + NZ - d) % NZ, c, :, own_rows, :]
            wait_in(block, zx_r.at[d])
        column_send(z)
        for direction in range(2):
            column_send(zat(direction, 1))
        column_wait(z)

    sib_copy(z).start()
    own_tiles(0)

    @pl.loop(1, last)
    def _(s):
        for f in range(2):
            @pl.when(c == 0)
            def _():
                for direction in range(2):
                    ring_wait(direction, s, f)
                    if direction == f:
                        ring_copy(direction, s + 1, f).start()
                    else:
                        @pl.when(s + 1 < last)
                        def _():
                            ring_copy(direction, s + 1, f).start()

            @pl.when(c == 1)
            def _():
                column_wait(zat(f, s))
                if f == 0:
                    column_send(zat(0, s + 1))
                else:
                    @pl.when(s + 1 < last)
                    def _():
                        column_send(zat(1, s + 1))

            if f == 0:
                sib_tiles(s - 1)
            else:
                planes(s, lambda zp: sib_copy(zp).start())
                own_tiles(s)
                pair_step(s - 1)
                planes(s - 1, pair_mix)

    sib_tiles(last - 1)

    @pl.when(c == 0)
    def _():
        ring_wait(0, last, 0)
        ring_wait(1, last, 1)

    @pl.when(c == 1)
    def _():
        column_wait((z + last) % NZ)

    sib_copy((z + last) % NZ).start()
    own_tiles(last)
    pair_step(last - 1)
    planes(last - 1, pair_mix)
    wait_in(rows.at[(z + last) % NZ, 1 - c], sib_r.at[(z + last) % NZ])
    tile_forward((z + last) % NZ, 1 - c)
    pair_send((z + last) % NZ)
    planes(last, pair_stats)
    scatter_copy(last).start()

    for d in range(1, NZ):
        wait_in(zparts.at[(z + NZ - d) % NZ], zs_r.at[d])
    top, total, inner = combine(lambda j: zparts[j], NZ)
    bparts[b] = jnp.concatenate([top, total, inner, inner], axis=0)

    def block_copy(d):
        return send(bparts.at[b], bparts.at[b], bp_s.at[d], bp_r.at[d], block_dev((b + d) % NB))

    for d in range(1, NB):
        block_copy(d).start()
    planes(last, pair_mix)
    for d in range(1, NB):
        wait_in(bparts.at[(b + NB - d) % NB], bp_r.at[d])
    top, total, inner = combine(lambda j: bparts[j], NB)
    inverse = 1.0 / total
    final[c, z] = jnp.concatenate([top, inverse, inner * inverse, inner], axis=0)

    def back_copy(d):
        return send(final.at[c, z], final.at[c, z], za_s.at[d], za_r.at[d], dev(y, (z + d) % NZ, x, c))

    for d in range(1, NZ):
        back_copy(d).start()
    for d in range(1, NZ):
        wait_in(final.at[c, (z + NZ - d) % NZ], za_r.at[d])
    final_copy = send(final.at[c], final.at[c], fin_s.at[0], fin_r.at[0], sibling)
    final_copy.start()

    def set_gain(zp, cp):
        share = jnp.exp(stats[zp, cp, 0:1, :] - final[cp, zp, 0:1, :]) * final[cp, zp, 1:2, :]
        gain[zp, cp] = jnp.concatenate([share, final[cp, zp, 2:3, :], share, share], axis=0)

    @pl.loop(0, NZ)
    def _(zp):
        set_gain(zp, c)
        share = jnp.exp(pairs[zp, 0:1, :] - final[c, zp, 0:1, :]) * final[c, zp, 1:2, :]
        qpart[zp] = jnp.transpose(mixed[zp, c] * share).astype(BF)

    def quant_copy(d):
        b_ = (b + d) % NB
        part = qpart.at[:, pl.ds(pl.multiple_of(b_ * own, own), own), :]
        return send(part, qplane.at[d - 1], qp_s.at[d], qp_r.at[d], block_dev(b_))

    for d in range(1, NB):
        quant_copy(d).start()

    wait_in(final.at[1 - c], fin_r.at[0])

    @pl.loop(0, NZ)
    def _(zp):
        set_gain(zp, 1 - c)

    def dp_copy(k):
        return send(gown_ref.at[k], gin.at[k], dp_s.at[k], dp_r.at[k], other_dp)

    def grad_chunk(k):
        ks = pl.ds(pl.multiple_of(k * CHUNK, CHUNK), CHUNK)
        out = jnp.zeros((CHUNK, width), F32)
        slopes = jnp.zeros((CHUNK, tile), F32)
        for zp in range(NZ):
            for cp in range(2):
                prob = expo[zp, cp, ks, :] * gain[zp, cp, 0:1, :]
                slope = prob * (align[zp, cp, ks, :] - gain[zp, cp, 1:2, :])
                out += jnp.dot(prob.astype(BF), rows[zp, cp, 1], preferred_element_type=F32)
                out += jnp.dot(slope.astype(BF), rows[zp, cp, 0], preferred_element_type=F32)
                slopes += slope
        moved = jnp.sum(slopes, axis=1, keepdims=True) * cb_ref[ks, :].astype(F32)
        gown_ref[k] = (out - moved).astype(BF)
        dp_copy(k).start()

    def z_copy(d):
        to = (z + d) % NZ
        return send(qsend.at[to], qz.at[d - 1], qz_s.at[d], qz_r.at[d], dev(y, to, x, c))

    @pl.loop(0, n_chunks)
    def _(k):
        grad_chunk(k)

    for d in range(1, NB):
        quant_copy(d).wait_recv()
    total = qpart[:, own_rows, :].astype(F32)
    for d in range(NB - 1):
        total += qplane[d].astype(F32)
    qsend[...] = total.astype(BF)
    for d in range(1, NZ):
        z_copy(d).start()

    for d in range(1, NB):
        block_copy(d).wait_send()
        quant_copy(d).wait_send()

    @pl.when(c == 0)
    def _():
        for d in range(1, NB):
            gather_copy(d, 1).wait_send()
        for f in range(2):
            @pl.loop(1, last)
            def _(s):
                for direction in range(2):
                    ring_copy(direction, s, f).wait_send()
            ring_copy(f, last, f).wait_send()

    @pl.when(c == 1)
    def _():
        for d in range(1, NZ):
            spread_copy(d).wait_send()

        @pl.loop(0, NZ)
        def _(zp):
            wait_out(rows.at[zp, c, :, 0:(NB - 1) * own, :], col_s.at[zp])

    for d in range(1, NZ):
        scatter_copy(d).wait_send()
        back_copy(d).wait_send()
    final_copy.wait_send()

    @pl.loop(0, NZ)
    def _(zp):
        sib_copy(zp).wait_send()
        pair_mix_copy(zp).wait_send()
        pair_stat_copy(zp).wait_send()

    @pl.loop(0, n_chunks)
    def _(k):
        dp_copy(k).wait()
        gin_ref[k] = gin[k]

    for d in range(1, NZ):
        z_copy(d).wait()
    quant = qsend[z].astype(F32)
    for d in range(NZ - 1):
        quant += qz[d].astype(F32)
    q_ref[...] = quant.astype(BF)


def body(latents, codebook, cotangent):
    own, width = latents.shape[1:]
    n_codes = codebook.shape[0]
    tile = NB * own
    n_chunks = n_codes // CHUNK
    n_tokens = own * lax.axis_size("code")
    scale = n_codes * lax.axis_size("code") * 1.0 / (lax.axis_size("dp") * n_tokens)
    vmem = pl.BlockSpec(memory_space=pltpu.VMEM)
    dma = pltpu.SemaphoreType.DMA
    half_ring = NZ // 2 + 1
    halves = jax.ShapeDtypeStruct((n_chunks, CHUNK, width), BF)
    quantized, here, there = pl.pallas_call(
        kernel,
        out_shape=(jax.ShapeDtypeStruct((own, width), BF), halves, halves),
        in_specs=[vmem] * 3,
        out_specs=(vmem, vmem, vmem),
        scratch_shapes=[
            pltpu.VMEM((NZ, NC, 2, tile, width), BF),
            pltpu.VMEM((NZ, NC, n_codes, tile), F32),
            pltpu.VMEM((NZ, NC, n_codes, tile), F32),
            pltpu.VMEM((NZ, NC, width, tile), F32),
            pltpu.VMEM((width, n_codes), BF),
            pltpu.VMEM((n_codes, tile), F32),
            pltpu.VMEM((NZ, NC, 4, tile), F32),
            pltpu.VMEM((NZ, 4, tile), F32),
            pltpu.VMEM((NZ, width, tile), BF),
            pltpu.VMEM((NZ, width, tile), BF),
            pltpu.VMEM((NZ, 4, tile), F32),
            pltpu.VMEM((NZ, 4, tile), F32),
            pltpu.VMEM((NB, 4, tile), F32),
            pltpu.VMEM((NC, NZ, 4, tile), F32),
            pltpu.VMEM((NZ, NC, 4, tile), F32),
            pltpu.VMEM((NZ, tile, width), BF),
            pltpu.VMEM((NB - 1, NZ, own, width), BF),
            pltpu.VMEM((NZ, own, width), BF),
            pltpu.VMEM((NZ - 1, own, width), BF),
            pltpu.VMEM((n_chunks, CHUNK, width), BF),
            dma((NB, 2)), dma((NB, 2)),
            dma((NZ,)), dma((NZ,)),
            dma((NZ,)), dma((NZ,)),
            dma((2, half_ring, 2)), dma((2, half_ring, 2)),
            dma((NZ,)), dma((NZ,)),
            dma((NZ,)), dma((NZ,)),
            dma((NZ,)), dma((NZ,)),
            dma((NZ,)), dma((NZ,)),
            dma((NB,)), dma((NB,)),
            dma((NZ,)), dma((NZ,)),
            dma((1,)), dma((1,)),
            dma((NB,)), dma((NB,)),
            dma((NZ,)), dma((NZ,)),
            dma((n_chunks,)), dma((n_chunks,)),
        ],
        compiler_params=pltpu.CompilerParams(
            collective_id=0, has_side_effects=True, vmem_limit_bytes=60 * 1024 * 1024,
        ),
        cost_estimate=pl.CostEstimate(
            flops=10 * n_codes * n_tokens * width, bytes_accessed=4 * n_codes * width,
            transcendentals=n_codes * n_tokens,
        ),
    )(latents[0], codebook, cotangent[0])
    grad = (here.astype(F32) + there.astype(F32)) * scale
    return quantized[None], grad.reshape(n_codes, width)


def solution(mesh):
    in_specs = (P("dp", "code", None), P("code", None), P("dp", "code", None))
    out_specs = (P("dp", "code", None), P("code", None))
    return jax.shard_map(body, mesh=mesh, in_specs=in_specs, out_specs=out_specs, check_vma=False)
```
